256 devices in a mesh: dp: 32 (over y, z), mp: 8 (over x, core).
Axes of the slice: x: 4, y: 4, z: 8, core: 2. Of those that a mesh axis runs over, the one named last changes fastest.
Arguments:
- gradient: bfloat16 [8, 96, 512, 512], P('mp', None, 'dp'), may hold values from -60 to 60
- owner_order: int32 [96], replicated, may hold values from 0 to 95, each once
- left_factor: bfloat16 [8, 96, 512, 512], P('mp', 'dp'), may hold values from -1 to 2, as said below
- right_factor: bfloat16 [8, 96, 512, 512], P('mp', 'dp'), may hold values from -1 to 2, as said below
- left_root: bfloat16 [8, 96, 512, 512], P('mp', 'dp'), may hold values from -1 to 2.5, as said below
- right_root: bfloat16 [8, 96, 512, 512], P('mp', 'dp'), may hold values from -1 to 2.5, as said below
Outputs:
- update: bfloat16 [8, 96, 512, 512], P('mp', None, 'dp')
- left_next: bfloat16 [8, 96, 512, 512], P('mp', 'dp')
- right_next: bfloat16 [8, 96, 512, 512], P('mp', 'dp')
The draws below stay inside these ranges and needn't reach their ends.
Inputs may be any that keep to these rules, and one draw needn't show every extreme that they name: `owner_order`: the block in slot p is owned by data index p // 3. `left_factor`: symmetric. `right_factor`: symmetric. `left_root`: symmetric. `right_root`: symmetric.
All inputs are finite; a program needn't handle non-finite values.
Results may differ from the reference program's by a relative error of at most 0.0049.
Values may be sent and summed in bfloat16 or wider, within the bound.
A program may use at most 64 MiB of HBM per device.

```python
import math
import jax
import jax.numpy as jnp
from jax import lax

BS = 512
NB = 96
N_MP = 8


def symmetric_matrix(off_values, main_diag, spread):
    size_last = off_values.shape[-1]
    mirrored = (off_values + jnp.swapaxes(off_values, -1, -2)) * spread
    row_index = lax_iota(size_last)
    diagonal_mask = row_index[:, None] == row_index[None, :]
    return jnp.where(diagonal_mask, main_diag[..., :, None], mirrored)


def lax_iota(length):
    return jnp.arange(length, dtype=jnp.int32)


def draw_gradient(key, part):
    key = jax.random.fold_in(key, 11)
    normal_key, row_key, column_key = jax.random.split(key, 3)
    full_shape = (N_MP, NB, BS, BS)
    values = jnp.clip(jax.random.normal(normal_key, full_shape, jnp.float32), -4.0, 4.0)
    row_scale = jnp.exp(jax.random.uniform(row_key, (N_MP, NB, BS, 1), jnp.float32, 0.0, math.log(10.0) / 2))
    column_scale = jnp.exp(jax.random.uniform(column_key, (N_MP, NB, 1, BS), jnp.float32, 0.0, math.log(10.0) / 2))
    shard_scale = jnp.linspace(1.0, 3.0, N_MP, dtype=jnp.float32).reshape(N_MP, 1, 1, 1)
    return (values * row_scale * column_scale * shard_scale / 3.0).astype(jnp.bfloat16)


def factor_like(key, low, high, logarithmic):
    diag_key, off_key = jax.random.split(key)
    full_shape = (N_MP, NB, BS, BS)
    if logarithmic > 0:
        main_diag = jnp.exp(jax.random.uniform(diag_key, (N_MP, NB, BS), jnp.float32, math.log(low), math.log(high)))
    else:
        main_diag = jax.random.uniform(diag_key, (N_MP, NB, BS), jnp.float32, low, high)
    return (off_key, main_diag, full_shape)


def draw_left_factor(key, part):
    key = jax.random.fold_in(key, 21)
    off_key, main_diag, full_shape = factor_like(key, 0.5, 1.5, 0)
    off_values = jnp.clip(jax.random.normal(off_key, full_shape, jnp.float32), -4.0, 4.0)
    return symmetric_matrix(off_values, main_diag, 0.2 / math.sqrt(BS)).astype(jnp.bfloat16)


def draw_right_factor(key, part):
    key = jax.random.fold_in(key, 22)
    off_key, main_diag, full_shape = factor_like(key, 0.5, 1.5, 0)
    off_values = jnp.clip(jax.random.normal(off_key, full_shape, jnp.float32), -4.0, 4.0)
    return symmetric_matrix(off_values, main_diag, 0.2 / math.sqrt(BS)).astype(jnp.bfloat16)


def draw_left_root(key, part):
    key = jax.random.fold_in(key, 23)
    off_key, main_diag, full_shape = factor_like(key, 0.5, 2.0, 1)
    off_values = jnp.clip(jax.random.normal(off_key, full_shape, jnp.float32), -4.0, 4.0)
    return symmetric_matrix(off_values, main_diag, 0.35 / math.sqrt(BS)).astype(jnp.bfloat16)


def draw_right_root(key, part):
    key = jax.random.fold_in(key, 24)
    off_key, main_diag, full_shape = factor_like(key, 0.5, 2.0, 1)
    off_values = jnp.clip(jax.random.normal(off_key, full_shape, jnp.float32), -4.0, 4.0)
    return symmetric_matrix(off_values, main_diag, 0.35 / math.sqrt(BS)).astype(jnp.bfloat16)


def setup_inputs(seed: int = 0) -> dict:
    key_list = jax.random.split(jax.random.key(seed), 7)
    return {
        "gradient": draw_gradient(jax.random.fold_in(key_list[6], 71), 0),
        "owner_order": jax.random.permutation(key_list[1], NB).astype(jnp.int32),
        "left_factor": draw_left_factor(jax.random.fold_in(key_list[6], 71), 0),
        "right_factor": draw_right_factor(jax.random.fold_in(key_list[6], 71), 0),
        "left_root": draw_left_root(jax.random.fold_in(key_list[6], 71), 0),
        "right_root": draw_right_root(jax.random.fold_in(key_list[6], 71), 0),
    }


factor_decay = 0.9
epsilon = 1e-06

def block_step(operands):
    grad_block, left_old, right_old, left_inv, right_inv = operands
    block_size = grad_block.shape[-1]
    gram_left = jnp.dot(grad_block, grad_block.T, preferred_element_type=jnp.float32)
    gram_right = jnp.dot(grad_block.T, grad_block, preferred_element_type=jnp.float32)
    coef = (1.0 - factor_decay) / block_size
    left_new = (factor_decay * left_old.astype(jnp.float32) + coef * gram_left).astype(jnp.bfloat16)
    right_new = (factor_decay * right_old.astype(jnp.float32) + coef * gram_right).astype(jnp.bfloat16)
    left_applied = jnp.dot(left_inv, grad_block, preferred_element_type=jnp.float32).astype(jnp.bfloat16)
    conditioned = jnp.dot(left_applied, right_inv, preferred_element_type=jnp.float32)
    grad_square = jnp.sum(jnp.square(grad_block.astype(jnp.float32)))
    cond_square = jnp.sum(conditioned * conditioned)
    return (left_new, right_new, conditioned, grad_square, cond_square)

def reference(gradient, owner_order, left_factor, right_factor, left_root, right_root):
    shards = gradient.shape[0]
    blocks = gradient.shape[1]
    block_size = gradient.shape[-1]
    owned = jnp.take(gradient, owner_order, axis=1)

    def flatten(array):
        return array.reshape(shards * blocks, block_size, block_size)
    left_new, right_new, conditioned, grad_square, cond_square = lax.map(block_step, (flatten(owned), flatten(left_factor), flatten(right_factor), flatten(left_root), flatten(right_root)))
    grad_total = lax.optimization_barrier(jnp.sum(grad_square.reshape(shards, blocks), axis=0))
    cond_total = lax.optimization_barrier(jnp.sum(cond_square.reshape(shards, blocks), axis=0))
    graft = jnp.sqrt((grad_total + epsilon) / (cond_total + epsilon))
    update_slot = (-graft[None, :, None, None] * conditioned.reshape(shards, blocks, block_size, block_size)).astype(jnp.bfloat16)
    places = jnp.zeros((blocks,), jnp.int32).at[owner_order].set(jnp.arange(blocks, dtype=jnp.int32))
    update = jnp.take(update_slot, places, axis=1)
    full_shape = (shards, blocks, block_size, block_size)
    return (update, left_new.reshape(full_shape), right_new.reshape(full_shape))
```

```python
import functools

import jax
import jax.numpy as jnp
from jax import lax
from jax.experimental import pallas as pl
from jax.experimental.pallas import tpu as pltpu
from jax.sharding import PartitionSpec as P

MESH = pl.DeviceIdType.MESH
factor_decay = 0.9
epsilon = 1e-06


def exchange_kernel(
    sizes,
    grad,
    order,
    left_old,
    right_old,
    left_inv,
    right_inv,
    returned,
    left_new,
    right_new,
    strips,
    stage,
    owned,
    lf,
    rf,
    lr,
    rr,
    cond,
    update,
    sums_out,
    sums_in,
    load_sem,
    out_send,
    out_recv,
    sum_send,
    sum_recv,
    back_send,
    back_recv,
):
    n_dp, n_mp, per, rows = sizes
    blocks = n_dp * per
    size = owned.shape[-1]
    dp = lax.axis_index("dp")
    mp = lax.axis_index("mp")
    coef = (1.0 - factor_decay) / size

    loads = [
        pltpu.make_async_copy(src, dst, load_sem.at[i])
        for i, (src, dst) in enumerate(
            (
                (grad.at[0], strips),
                (left_inv.at[0], lr),
                (right_inv.at[0], rr),
                (left_old.at[0], lf),
                (right_old.at[0], rf),
            )
        )
    ]
    loads[0].start()

    barrier = pltpu.get_barrier_semaphore()

    @pl.loop(1, n_dp)
    def _(j):
        pl.semaphore_signal(
            barrier, inc=1, device_id=(lax.rem(dp + j, n_dp), mp), device_id_type=MESH
        )

    @pl.loop(1, n_mp)
    def _(j):
        pl.semaphore_signal(
            barrier, inc=1, device_id=(dp, lax.rem(mp + j, n_mp)), device_id_type=MESH
        )

    for load in loads[1:]:
        load.start()
    loads[0].wait()

    @pl.loop(0, blocks)
    def _(p):
        stage[p] = strips[order[p]]

    my_rows = pl.ds(pl.multiple_of(dp * rows, rows), rows)
    for k in range(per):
        owned[k, my_rows, :] = stage[dp * per + k]

    pl.semaphore_wait(barrier, n_dp - 1 + n_mp - 1)

    @pl.loop(0, per)
    def _(k):
        @pl.loop(1, n_dp)
        def _(j):
            dst = lax.rem(dp + j, n_dp)
            pltpu.make_async_remote_copy(
                src_ref=stage.at[dst * per + k],
                dst_ref=owned.at[k, my_rows],
                send_sem=out_send,
                recv_sem=out_recv.at[k],
                device_id=(dst, mp),
                device_id_type=MESH,
            ).start()

    for load in loads[1:]:
        load.wait()

    @pl.loop(0, per)
    def _(k):
        others = owned.at[k, pl.ds(0, (n_dp - 1) * rows)]
        pltpu.make_async_copy(others, others, out_recv.at[k]).wait()

        applied = jnp.dot(lr[k], owned[k], preferred_element_type=jnp.float32).astype(jnp.bfloat16)
        cond[...] = jnp.dot(applied, rr[k], preferred_element_type=jnp.float32)
        wide = owned[k].astype(jnp.float32)
        grad_square = jnp.sum(wide * wide)
        cond_square = jnp.sum(cond[...] * cond[...])
        row = lax.broadcasted_iota(jnp.int32, (8, 128), 0)
        mine = jnp.where(row == 0, grad_square, cond_square)
        sums_out[k] = mine
        sums_in[k, mp] = mine

        @pl.loop(1, n_mp)
        def _(j):
            pltpu.make_async_remote_copy(
                src_ref=sums_out.at[k],
                dst_ref=sums_in.at[k, mp],
                send_sem=sum_send,
                recv_sem=sum_recv.at[k],
                device_id=(dp, lax.rem(mp + j, n_mp)),
                device_id_type=MESH,
            ).start()

        block = owned[k]
        gram_left = lax.dot_general(
            block, block, (((1,), (1,)), ((), ())), preferred_element_type=jnp.float32
        )
        left_new[k] = (factor_decay * lf[k].astype(jnp.float32) + coef * gram_left).astype(
            jnp.bfloat16
        )
        gram_right = lax.dot_general(
            block, block, (((0,), (0,)), ((), ())), preferred_element_type=jnp.float32
        )
        right_new[k] = (factor_decay * rf[k].astype(jnp.float32) + coef * gram_right).astype(
            jnp.bfloat16
        )

        parts = sums_in.at[k, pl.ds(0, n_mp - 1)]
        pltpu.make_async_copy(parts, parts, sum_recv.at[k]).wait()
        total = jnp.sum(sums_in[k], axis=0)
        graft = jnp.sqrt((total[0:1, 0:1] + epsilon) / (total[1:2, 0:1] + epsilon))
        update[k] = (-graft * cond[...]).astype(jnp.bfloat16)
        returned[dp * per + k] = update[k, my_rows, :]

        @pl.loop(1, n_dp)
        def _(j):
            dst = lax.rem(dp + j, n_dp)
            pltpu.make_async_remote_copy(
                src_ref=update.at[k, pl.ds(pl.multiple_of(dst * rows, rows), rows)],
                dst_ref=returned.at[dp * per + k],
                send_sem=back_send,
                recv_sem=back_recv,
                device_id=(dst, mp),
                device_id_type=MESH,
            ).start()

    others = (n_dp - 1) * per
    for sem in (out_send, back_send):
        pltpu.make_async_copy(
            stage.at[pl.ds(0, others)], stage.at[pl.ds(0, others)], sem
        ).wait()
    for k in range(per):
        parts = sums_in.at[k, pl.ds(0, n_mp - 1)]
        pltpu.make_async_copy(parts, parts, sum_send).wait()
    arrived = returned.at[pl.ds(0, others)]
    pltpu.make_async_copy(arrived, arrived, back_recv).wait()


def finish_kernel(order, returned, left, right, update, left_next, right_next, placed, sem):
    copies = [
        pltpu.make_async_copy(left, left_next.at[0], sem.at[0]),
        pltpu.make_async_copy(right, right_next.at[0], sem.at[1]),
        pltpu.make_async_copy(placed, update.at[0], sem.at[2]),
    ]
    copies[0].start()
    copies[1].start()

    @pl.loop(0, placed.shape[0])
    def _(p):
        placed[order[p]] = returned[p]

    copies[2].start()
    for copy in copies:
        copy.wait()


def body(n_dp, n_mp, gradient, owner_order, left_factor, right_factor, left_root, right_root):
    _, blocks, rows, size = gradient.shape
    per = left_factor.shape[1]
    bf16, f32 = jnp.bfloat16, jnp.float32
    strips = (blocks, rows, size)
    squares = (per, size, size)
    any_spec = pl.BlockSpec(memory_space=pl.ANY)
    smem_spec = pl.BlockSpec(memory_space=pltpu.SMEM)
    vmem_spec = pl.BlockSpec(memory_space=pltpu.VMEM)
    far = lambda x: pltpu.with_memory_space_constraint(x, pltpu.HBM)
    macs = 4 * per * size**3
    moved = gradient.size * 2
    returned, left_new, right_new = pl.pallas_call(
        functools.partial(exchange_kernel, (n_dp, n_mp, per, rows)),
        out_shape=[
            pltpu.VMEM(strips, bf16),
            pltpu.VMEM(squares, bf16),
            pltpu.VMEM(squares, bf16),
        ],
        in_specs=[any_spec, smem_spec] + [any_spec] * 4,
        out_specs=[vmem_spec] * 3,
        scratch_shapes=[
            pltpu.VMEM(strips, bf16),
            pltpu.VMEM(strips, bf16),
            pltpu.VMEM(squares, bf16),
            pltpu.VMEM(squares, bf16),
            pltpu.VMEM(squares, bf16),
            pltpu.VMEM(squares, bf16),
            pltpu.VMEM(squares, bf16),
            pltpu.VMEM((size, size), f32),
            pltpu.VMEM(squares, bf16),
            pltpu.VMEM((per, 8, 128), f32),
            pltpu.VMEM((per, n_mp, 8, 128), f32),
            pltpu.SemaphoreType.DMA((5,)),
            pltpu.SemaphoreType.DMA(()),
            pltpu.SemaphoreType.DMA((per,)),
            pltpu.SemaphoreType.DMA(()),
            pltpu.SemaphoreType.DMA((per,)),
            pltpu.SemaphoreType.DMA(()),
            pltpu.SemaphoreType.DMA(()),
        ],
        compiler_params=pltpu.CompilerParams(
            collective_id=0, has_side_effects=True, vmem_limit_bytes=40 << 20
        ),
        cost_estimate=pl.CostEstimate(
            flops=2 * macs, bytes_accessed=8 * moved, transcendentals=0
        ),
        name="exchange",
    )(
        far(gradient),
        owner_order,
        far(left_factor),
        far(right_factor),
        far(left_root),
        far(right_root),
    )

    keep = lambda x: pltpu.with_memory_space_constraint(x, pltpu.VMEM)
    return pl.pallas_call(
        finish_kernel,
        out_shape=[
            jax.ShapeDtypeStruct(gradient.shape, bf16),
            jax.ShapeDtypeStruct((1,) + squares, bf16),
            jax.ShapeDtypeStruct((1,) + squares, bf16),
        ],
        in_specs=[smem_spec] + [vmem_spec] * 3,
        out_specs=[any_spec] * 3,
        scratch_shapes=[pltpu.VMEM(strips, bf16), pltpu.SemaphoreType.DMA((3,))],
        compiler_params=pltpu.CompilerParams(vmem_limit_bytes=16 << 20),
        cost_estimate=pl.CostEstimate(flops=0, bytes_accessed=6 * moved, transcendentals=0),
        name="finish",
    )(owner_order, keep(returned), keep(left_new), keep(right_new))


def solution(mesh):
    return jax.shard_map(
        functools.partial(body, mesh.shape["dp"], mesh.shape["mp"]),
        mesh=mesh,
        in_specs=(
            P("mp", None, "dp", None),
            P(),
            P("mp", "dp", None, None),
            P("mp", "dp", None, None),
            P("mp", "dp", None, None),
            P("mp", "dp", None, None),
        ),
        out_specs=(P("mp", None, "dp", None), P("mp", "dp", None, None), P("mp", "dp", None, None)),
        check_vma=False,
    )
```

```python
import functools

import jax
import jax.numpy as jnp
from jax import lax
from jax.experimental import pallas as pl
from jax.experimental.pallas import tpu as pltpu
from jax.sharding import PartitionSpec as P

MESH = pl.DeviceIdType.MESH
factor_decay = 0.9
epsilon = 1e-06
RING = 8


def exchange_kernel(
    sizes,
    grad,
    order,
    left_old,
    right_old,
    left_inv,
    right_inv,
    returned,
    left_new,
    right_new,
    strips,
    stage,
    owned,
    slots,
    lf,
    rf,
    lr,
    rr,
    cond,
    update,
    sums_out,
    sums_in,
    news,
    load_sem,
    out_send,
    out_recv,
    sum_send,
    sum_recv,
    back_send,
    back_recv,
):
    n_dp, per, rows = sizes
    n_y, n_z = n_dp // RING, RING
    blocks = n_dp * per
    size = owned.shape[-1]
    dp = lax.axis_index("dp")
    mp = lax.axis_index("mp")
    coef = (1.0 - factor_decay) / size
    y, z = dp // n_z, lax.rem(dp, n_z)
    x, core = mp // 2, lax.rem(mp, 2)
    partners = (2 * x + 1 - core, 2 * (x + 1 - 2 * lax.rem(x, 2)) + core, 2 * (3 - x) + core)

    def peer(dy, dz):
        return lax.rem(y + dy, n_y) * n_z + lax.rem(z + dz, n_z)

    loads = [
        pltpu.make_async_copy(src, dst, load_sem.at[i])
        for i, (src, dst) in enumerate(
            (
                (order, slots),
                (grad.at[0], strips),
                (left_inv.at[0], lr),
                (right_inv.at[0], rr),
                (left_old.at[0], lf),
                (right_old.at[0], rf),
            )
        )
    ]
    loads[0].start()
    loads[1].start()

    barrier = pltpu.get_barrier_semaphore()

    def signal(sem, dev):
        pl.semaphore_signal(sem, inc=1, device_id=dev, device_id_type=MESH)

    for dy in (2, 1, n_y - 1):
        signal(barrier, (peer(dy, 0), mp))
    for dz in (1, n_z - 1):
        signal(barrier, (peer(0, dz), mp))
    for partner in partners:
        signal(barrier, (dp, partner))

    for load in loads[2:]:
        load.start()
    loads[0].wait()
    loads[1].wait()

    my_rows = pl.ds(pl.multiple_of(dp * rows, rows), rows)

    def gather(k):
        @pl.loop(0, n_dp, unroll=4)
        def _(d):
            stage[d * per + k] = strips[slots[d * per + k]]

        owned[k, my_rows, :] = stage[dp * per + k]

    def send(k, dst):
        pltpu.make_async_remote_copy(
            src_ref=stage.at[dst * per + k],
            dst_ref=owned.at[k, my_rows],
            send_sem=out_send,
            recv_sem=out_recv.at[k],
            device_id=(dst, mp),
            device_id_type=MESH,
        ).start()

    def send_near(k):
        for dz in (1, n_z - 1):
            send(k, peer(0, dz))
        for dy in range(1, n_y):
            send(k, peer(dy, 0))

    def relay(step):
        for dz in (1, n_z - 1):
            signal(news.at[step], (peer(0, dz), mp))

    gather(0)
    pl.semaphore_wait(barrier, n_y - 1 + 2 + len(partners))
    relay(0)
    send_near(0)
    for k in range(1, per):
        gather(k)
        send_near(k)
    for step in range(n_z // 2):
        pl.semaphore_wait(news.at[step], 2)
        if step + 1 < n_z // 2:
            relay(step + 1)
        dist = step + 1
        sides = (dist, n_z - dist) if 2 * dist < n_z else (dist,)
        for dz in sides:

            @pl.loop(1, n_y)
            def _(dy):
                send(0, peer(dy, dz))

        if dist + 1 <= n_z // 2:
            for dz in (dist + 1, n_z - dist - 1)[: 2 if 2 * dist + 2 < n_z else 1]:
                send(0, peer(0, dz))

    for k in range(1, per):

        @pl.loop(2, n_z - 1)
        def _(dz):
            send(k, peer(0, dz))

        @pl.loop(0, (n_y - 1) * (n_z - 1))
        def _(i):
            send(k, peer(1 + i // (n_z - 1), 1 + lax.rem(i, n_z - 1)))

    for load in loads[2:]:
        load.wait()

    @pl.loop(0, per)
    def _(k):
        others = owned.at[k, pl.ds(0, (n_dp - 1) * rows)]
        pltpu.make_async_copy(others, others, out_recv.at[k]).wait()

        applied = jnp.dot(lr[k], owned[k], preferred_element_type=jnp.float32).astype(jnp.bfloat16)
        cond[...] = jnp.dot(applied, rr[k], preferred_element_type=jnp.float32)
        wide = owned[k].astype(jnp.float32)
        grad_square = jnp.sum(wide * wide)
        cond_square = jnp.sum(cond[...] * cond[...])
        row = lax.broadcasted_iota(jnp.int32, (8, 128), 0)
        mine = jnp.where(row == 0, grad_square, cond_square)
        def trade(step, value):
            sums_out[k, step] = value
            copy = pltpu.make_async_remote_copy(
                src_ref=sums_out.at[k, step],
                dst_ref=sums_in.at[k, step],
                send_sem=sum_send.at[k, step],
                recv_sem=sum_recv.at[k, step],
                device_id=(dp, partners[step]),
                device_id_type=MESH,
            )
            copy.start()
            return copy

        copy = trade(0, mine)

        block = owned[k]
        gram_left = lax.dot_general(
            block, block, (((1,), (1,)), ((), ())), preferred_element_type=jnp.float32
        )
        left_new[k] = (factor_decay * lf[k].astype(jnp.float32) + coef * gram_left).astype(
            jnp.bfloat16
        )
        gram_right = lax.dot_general(
            block, block, (((0,), (0,)), ((), ())), preferred_element_type=jnp.float32
        )
        right_new[k] = (factor_decay * rf[k].astype(jnp.float32) + coef * gram_right).astype(
            jnp.bfloat16
        )

        for step in range(len(partners)):
            copy.wait()
            total = sums_out[k, step] + sums_in[k, step]
            if step + 1 < len(partners):
                copy = trade(step + 1, total)
        graft = jnp.sqrt((total[0:1, 0:1] + epsilon) / (total[1:2, 0:1] + epsilon))
        update[k] = (-graft * cond[...]).astype(jnp.bfloat16)
        returned[dp * per + k] = update[k, my_rows, :]

        @pl.loop(1, n_dp)
        def _(j):
            dst = lax.rem(dp + j, n_dp)
            pltpu.make_async_remote_copy(
                src_ref=update.at[k, pl.ds(pl.multiple_of(dst * rows, rows), rows)],
                dst_ref=returned.at[dp * per + k],
                send_sem=back_send,
                recv_sem=back_recv,
                device_id=(dst, mp),
                device_id_type=MESH,
            ).start()

    others = (n_dp - 1) * per
    for sem in (out_send, back_send):
        pltpu.make_async_copy(
            stage.at[pl.ds(0, others)], stage.at[pl.ds(0, others)], sem
        ).wait()
    arrived = returned.at[pl.ds(0, others)]
    pltpu.make_async_copy(arrived, arrived, back_recv).wait()


def finish_kernel(
    order, returned, left, right, update, left_next, right_next, slots, placed, sem
):
    copies = [
        pltpu.make_async_copy(order, slots, sem.at[0]),
        pltpu.make_async_copy(left, left_next.at[0], sem.at[1]),
        pltpu.make_async_copy(right, right_next.at[0], sem.at[2]),
        pltpu.make_async_copy(placed, update.at[0], sem.at[3]),
    ]
    for copy in copies[:3]:
        copy.start()
    copies[0].wait()

    @pl.loop(0, placed.shape[0], unroll=4)
    def _(p):
        placed[slots[p]] = returned[p]

    copies[3].start()
    for copy in copies[1:]:
        copy.wait()


def body(n_dp, gradient, owner_order, left_factor, right_factor, left_root, right_root):
    _, blocks, rows, size = gradient.shape
    per = left_factor.shape[1]
    bf16, f32 = jnp.bfloat16, jnp.float32
    strips = (blocks, rows, size)
    squares = (per, size, size)
    any_spec = pl.BlockSpec(memory_space=pl.ANY)
    vmem_spec = pl.BlockSpec(memory_space=pltpu.VMEM)
    far = lambda x: pltpu.with_memory_space_constraint(x, pltpu.HBM)
    macs = 4 * per * size**3
    moved = gradient.size * 2
    returned, left_new, right_new = pl.pallas_call(
        functools.partial(exchange_kernel, (n_dp, per, rows)),
        out_shape=[
            pltpu.VMEM(strips, bf16),
            pltpu.VMEM(squares, bf16),
            pltpu.VMEM(squares, bf16),
        ],
        in_specs=[any_spec] * 6,
        out_specs=[vmem_spec] * 3,
        scratch_shapes=[
            pltpu.VMEM(strips, bf16),
            pltpu.VMEM(strips, bf16),
            pltpu.VMEM(squares, bf16),
            pltpu.SMEM((blocks,), jnp.int32),
            pltpu.VMEM(squares, bf16),
            pltpu.VMEM(squares, bf16),
            pltpu.VMEM(squares, bf16),
            pltpu.VMEM(squares, bf16),
            pltpu.VMEM((size, size), f32),
            pltpu.VMEM(squares, bf16),
            pltpu.VMEM((per, 3, 8, 128), f32),
            pltpu.VMEM((per, 3, 8, 128), f32),
            pltpu.SemaphoreType.REGULAR((RING // 2,)),
            pltpu.SemaphoreType.DMA((6,)),
            pltpu.SemaphoreType.DMA(()),
            pltpu.SemaphoreType.DMA((per,)),
            pltpu.SemaphoreType.DMA((per, 3)),
            pltpu.SemaphoreType.DMA((per, 3)),
            pltpu.SemaphoreType.DMA(()),
            pltpu.SemaphoreType.DMA(()),
        ],
        compiler_params=pltpu.CompilerParams(
            collective_id=0, has_side_effects=True, vmem_limit_bytes=40 << 20
        ),
        cost_estimate=pl.CostEstimate(
            flops=2 * macs, bytes_accessed=8 * moved, transcendentals=0
        ),
        name="exchange",
    )(
        far(gradient),
        far(owner_order),
        far(left_factor),
        far(right_factor),
        far(left_root),
        far(right_root),
    )

    keep = lambda x: pltpu.with_memory_space_constraint(x, pltpu.VMEM)
    return pl.pallas_call(
        finish_kernel,
        out_shape=[
            jax.ShapeDtypeStruct(gradient.shape, bf16),
            jax.ShapeDtypeStruct((1,) + squares, bf16),
            jax.ShapeDtypeStruct((1,) + squares, bf16),
        ],
        in_specs=[any_spec] + [vmem_spec] * 3,
        out_specs=[any_spec] * 3,
        scratch_shapes=[
            pltpu.SMEM((blocks,), jnp.int32),
            pltpu.VMEM(strips, bf16),
            pltpu.SemaphoreType.DMA((4,)),
        ],
        compiler_params=pltpu.CompilerParams(vmem_limit_bytes=16 << 20),
        cost_estimate=pl.CostEstimate(flops=0, bytes_accessed=6 * moved, transcendentals=0),
        name="finish",
    )(far(owner_order), keep(returned), keep(left_new), keep(right_new))


def solution(mesh):
    return jax.shard_map(
        functools.partial(body, mesh.shape["dp"]),
        mesh=mesh,
        in_specs=(
            P("mp", None, "dp", None),
            P(),
            P("mp", "dp", None, None),
            P("mp", "dp", None, None),
            P("mp", "dp", None, None),
            P("mp", "dp", None, None),
        ),
        out_specs=(P("mp", None, "dp", None), P("mp", "dp", None, None), P("mp", "dp", None, None)),
        check_vma=False,
    )
```

```python
import functools

import jax
import jax.numpy as jnp
from jax import lax
from jax.experimental import pallas as pl
from jax.experimental.pallas import tpu as pltpu
from jax.sharding import PartitionSpec as P

MESH = pl.DeviceIdType.MESH
factor_decay = 0.9
epsilon = 1e-06
RING = 8
EARLY = 3


def exchange_kernel(
    sizes,
    grad,
    order,
    left_old,
    right_old,
    left_inv,
    right_inv,
    returned,
    left_new,
    right_new,
    strips,
    stage,
    owned,
    slots,
    lf,
    rf,
    lr,
    rr,
    cond,
    update,
    sums_out,
    sums_in,
    news,
    load_sem,
    out_send,
    out_recv,
    sum_send,
    sum_recv,
    back_send,
    back_recv,
):
    n_dp, per, rows = sizes
    n_y, n_z = n_dp // RING, RING
    blocks = n_dp * per
    size = owned.shape[-1]
    dp = lax.axis_index("dp")
    mp = lax.axis_index("mp")
    coef = (1.0 - factor_decay) / size
    y, z = dp // n_z, lax.rem(dp, n_z)
    x, core = mp // 2, lax.rem(mp, 2)
    partners = (2 * x + 1 - core, 2 * (x + 1 - 2 * lax.rem(x, 2)) + core, 2 * (3 - x) + core)

    def peer(dy, dz):
        return lax.rem(y + dy, n_y) * n_z + lax.rem(z + dz, n_z)

    loads = [
        pltpu.make_async_copy(src, dst, load_sem.at[i])
        for i, (src, dst) in enumerate(
            (
                (order, slots),
                (grad.at[0], strips),
                (left_inv.at[0], lr),
                (right_inv.at[0], rr),
                (left_old.at[0], lf),
                (right_old.at[0], rf),
            )
        )
    ]
    loads[0].start()
    loads[1].start()

    barrier = pltpu.get_barrier_semaphore()

    def signal(sem, dev):
        pl.semaphore_signal(sem, inc=1, device_id=dev, device_id_type=MESH)

    for dy in (2, 1, n_y - 1):
        signal(barrier, (peer(dy, 0), mp))
    for dz in (1, n_z - 1):
        signal(barrier, (peer(0, dz), mp))
    for partner in partners:
        signal(barrier, (dp, partner))

    for load in loads[2:]:
        load.start()
    loads[0].wait()
    loads[1].wait()

    my_rows = pl.ds(pl.multiple_of(dp * rows, rows), rows)

    def gather(k):
        @pl.loop(0, n_dp, unroll=4)
        def _(d):
            stage[d * per + k] = strips[slots[d * per + k]]

        owned[k, my_rows, :] = stage[dp * per + k]

    def send(k, dst):
        pltpu.make_async_remote_copy(
            src_ref=stage.at[dst * per + k],
            dst_ref=owned.at[k, my_rows],
            send_sem=out_send,
            recv_sem=out_recv.at[k],
            device_id=(dst, mp),
            device_id_type=MESH,
        ).start()

    def send_near(k):
        for dz in (1, n_z - 1):
            send(k, peer(0, dz))
        for dy in range(1, n_y):
            send(k, peer(dy, 0))

    def relay(step):
        for dz in (1, n_z - 1):
            signal(news.at[step], (peer(0, dz), mp))

    gather(0)
    pl.semaphore_wait(barrier, n_y - 1 + 2 + len(partners))
    relay(0)
    send_near(0)
    for k in range(1, per):
        gather(k)
        send_near(k)
    for step in range(n_z // 2):
        pl.semaphore_wait(news.at[step], 2)
        if step + 1 < n_z // 2:
            relay(step + 1)
        dist = step + 1
        sides = (dist, n_z - dist) if 2 * dist < n_z else (dist,)
        for dz in sides:

            @pl.loop(1, n_y)
            def _(dy):
                send(0, peer(dy, dz))

        if dist + 1 <= n_z // 2:
            for dz in (dist + 1, n_z - dist - 1)[: 2 if 2 * dist + 2 < n_z else 1]:
                send(0, peer(0, dz))

    for k in range(1, per):

        @pl.loop(2, n_z - 1)
        def _(dz):
            send(k, peer(0, dz))

        @pl.loop(0, (n_y - 1) * (n_z - 1))
        def _(i):
            send(k, peer(1 + i // (n_z - 1), 1 + lax.rem(i, n_z - 1)))

    for load in loads[2:]:
        load.wait()

    @pl.loop(0, per)
    def _(k):
        others = owned.at[k, pl.ds(0, (n_dp - 1) * rows)]
        pltpu.make_async_copy(others, others, out_recv.at[k]).wait()

        applied = jnp.dot(lr[k], owned[k], preferred_element_type=jnp.float32).astype(jnp.bfloat16)
        cond[...] = jnp.dot(applied, rr[k], preferred_element_type=jnp.float32)
        wide = owned[k].astype(jnp.float32)
        grad_square = jnp.sum(wide * wide)
        cond_square = jnp.sum(cond[...] * cond[...])
        row = lax.broadcasted_iota(jnp.int32, (8, 128), 0)
        mine = jnp.where(row == 0, grad_square, cond_square)
        def trade(step, value):
            sums_out[k, step] = value
            copy = pltpu.make_async_remote_copy(
                src_ref=sums_out.at[k, step],
                dst_ref=sums_in.at[k, step],
                send_sem=sum_send.at[k, step],
                recv_sem=sum_recv.at[k, step],
                device_id=(dp, partners[step]),
                device_id_type=MESH,
            )
            copy.start()
            return copy

        copy = trade(0, mine)

        block = owned[k]
        gram_left = lax.dot_general(
            block, block, (((1,), (1,)), ((), ())), preferred_element_type=jnp.float32
        )
        left_new[k] = (factor_decay * lf[k].astype(jnp.float32) + coef * gram_left).astype(
            jnp.bfloat16
        )
        gram_right = lax.dot_general(
            block, block, (((0,), (0,)), ((), ())), preferred_element_type=jnp.float32
        )
        right_new[k] = (factor_decay * rf[k].astype(jnp.float32) + coef * gram_right).astype(
            jnp.bfloat16
        )

        for step in range(len(partners)):
            copy.wait()
            total = sums_out[k, step] + sums_in[k, step]
            if step + 1 < len(partners):
                copy = trade(step + 1, total)
        graft = jnp.sqrt((total[0:1, 0:1] + epsilon) / (total[1:2, 0:1] + epsilon))
        update[k] = (-graft * cond[...]).astype(jnp.bfloat16)
        returned[dp * per + k] = update[k, my_rows, :]

        def send_back(dst):
            pltpu.make_async_remote_copy(
                src_ref=update.at[k, pl.ds(pl.multiple_of(dst * rows, rows), rows)],
                dst_ref=returned.at[dp * per + k],
                send_sem=back_send,
                recv_sem=back_recv,
                device_id=(dst, mp),
                device_id_type=MESH,
            ).start()

        for chosen in (
            lambda yy, zz: (zz < EARLY) & (yy == 0),
            lambda yy, zz: (zz < EARLY) & (yy != 0),
            lambda yy, zz: zz >= EARLY,
        ):

            @pl.loop(1, n_dp)
            def _(j):
                dst = lax.rem(dp + j, n_dp)

                @pl.when(chosen(dst // n_z, lax.rem(dst, n_z)))
                def _():
                    send_back(dst)

    others = (n_dp - 1) * per
    for sem in (out_send, back_send):
        pltpu.make_async_copy(
            stage.at[pl.ds(0, others)], stage.at[pl.ds(0, others)], sem
        ).wait()
    arrived = returned.at[pl.ds(0, others)]
    pltpu.make_async_copy(arrived, arrived, back_recv).wait()


def finish_kernel(
    order, returned, left, right, update, left_next, right_next, slots, placed, sem
):
    copies = [
        pltpu.make_async_copy(order, slots, sem.at[0]),
        pltpu.make_async_copy(left, left_next.at[0], sem.at[1]),
        pltpu.make_async_copy(right, right_next.at[0], sem.at[2]),
        pltpu.make_async_copy(placed, update.at[0], sem.at[3]),
    ]
    for copy in copies[:3]:
        copy.start()
    copies[0].wait()

    @pl.loop(0, placed.shape[0], unroll=4)
    def _(p):
        placed[slots[p]] = returned[p]

    copies[3].start()
    for copy in copies[1:]:
        copy.wait()


def body(n_dp, gradient, owner_order, left_factor, right_factor, left_root, right_root):
    _, blocks, rows, size = gradient.shape
    per = left_factor.shape[1]
    bf16, f32 = jnp.bfloat16, jnp.float32
    strips = (blocks, rows, size)
    squares = (per, size, size)
    any_spec = pl.BlockSpec(memory_space=pl.ANY)
    vmem_spec = pl.BlockSpec(memory_space=pltpu.VMEM)
    far = lambda x: pltpu.with_memory_space_constraint(x, pltpu.HBM)
    macs = 4 * per * size**3
    moved = gradient.size * 2
    returned, left_new, right_new = pl.pallas_call(
        functools.partial(exchange_kernel, (n_dp, per, rows)),
        out_shape=[
            pltpu.VMEM(strips, bf16),
            pltpu.VMEM(squares, bf16),
            pltpu.VMEM(squares, bf16),
        ],
        in_specs=[any_spec] * 6,
        out_specs=[vmem_spec] * 3,
        scratch_shapes=[
            pltpu.VMEM(strips, bf16),
            pltpu.VMEM(strips, bf16),
            pltpu.VMEM(squares, bf16),
            pltpu.SMEM((blocks,), jnp.int32),
            pltpu.VMEM(squares, bf16),
            pltpu.VMEM(squares, bf16),
            pltpu.VMEM(squares, bf16),
            pltpu.VMEM(squares, bf16),
            pltpu.VMEM((size, size), f32),
            pltpu.VMEM(squares, bf16),
            pltpu.VMEM((per, 3, 8, 128), f32),
            pltpu.VMEM((per, 3, 8, 128), f32),
            pltpu.SemaphoreType.REGULAR((RING // 2,)),
            pltpu.SemaphoreType.DMA((6,)),
            pltpu.SemaphoreType.DMA(()),
            pltpu.SemaphoreType.DMA((per,)),
            pltpu.SemaphoreType.DMA((per, 3)),
            pltpu.SemaphoreType.DMA((per, 3)),
            pltpu.SemaphoreType.DMA(()),
            pltpu.SemaphoreType.DMA(()),
        ],
        compiler_params=pltpu.CompilerParams(
            collective_id=0, has_side_effects=True, vmem_limit_bytes=40 << 20
        ),
        cost_estimate=pl.CostEstimate(
            flops=2 * macs, bytes_accessed=8 * moved, transcendentals=0
        ),
        name="exchange",
    )(
        far(gradient),
        far(owner_order),
        far(left_factor),
        far(right_factor),
        far(left_root),
        far(right_root),
    )

    keep = lambda x: pltpu.with_memory_space_constraint(x, pltpu.VMEM)
    return pl.pallas_call(
        finish_kernel,
        out_shape=[
            jax.ShapeDtypeStruct(gradient.shape, bf16),
            jax.ShapeDtypeStruct((1,) + squares, bf16),
            jax.ShapeDtypeStruct((1,) + squares, bf16),
        ],
        in_specs=[any_spec] + [vmem_spec] * 3,
        out_specs=[any_spec] * 3,
        scratch_shapes=[
            pltpu.SMEM((blocks,), jnp.int32),
            pltpu.VMEM(strips, bf16),
            pltpu.SemaphoreType.DMA((4,)),
        ],
        compiler_params=pltpu.CompilerParams(vmem_limit_bytes=16 << 20),
        cost_estimate=pl.CostEstimate(flops=0, bytes_accessed=6 * moved, transcendentals=0),
        name="finish",
    )(far(owner_order), keep(returned), keep(left_new), keep(right_new))


def solution(mesh):
    return jax.shard_map(
        functools.partial(body, mesh.shape["dp"]),
        mesh=mesh,
        in_specs=(
            P("mp", None, "dp", None),
            P(),
            P("mp", "dp", None, None),
            P("mp", "dp", None, None),
            P("mp", "dp", None, None),
            P("mp", "dp", None, None),
        ),
        out_specs=(P("mp", None, "dp", None), P("mp", "dp", None, None), P("mp", "dp", None, None)),
        check_vma=False,
    )
```

```python
import functools

import jax
import jax.numpy as jnp
from jax import lax
from jax.experimental import pallas as pl
from jax.experimental.pallas import tpu as pltpu
from jax.sharding import PartitionSpec as P

MESH = pl.DeviceIdType.MESH
factor_decay = 0.9
epsilon = 1e-06
RING = 8
EARLY = 3


def exchange_kernel(
    sizes,
    grad,
    order,
    left_old,
    right_old,
    left_inv,
    right_inv,
    returned,
    left_new,
    right_new,
    strips,
    stage,
    owned,
    slots,
    lf,
    rf,
    lr,
    rr,
    cond,
    update,
    sums_out,
    sums_in,
    news,
    load_sem,
    out_send,
    out_recv,
    sum_send,
    sum_recv,
    back_send,
    back_recv,
):
    n_dp, per, rows = sizes
    n_y, n_z = n_dp // RING, RING
    blocks = n_dp * per
    size = owned.shape[-1]
    dp = lax.axis_index("dp")
    mp = lax.axis_index("mp")
    coef = (1.0 - factor_decay) / size
    y, z = dp // n_z, lax.rem(dp, n_z)
    x, core = mp // 2, lax.rem(mp, 2)
    partners = (2 * x + 1 - core, 2 * (x + 1 - 2 * lax.rem(x, 2)) + core, 2 * (3 - x) + core)

    def peer(dy, dz):
        return lax.rem(y + dy, n_y) * n_z + lax.rem(z + dz, n_z)

    loads = [
        pltpu.make_async_copy(src, dst, load_sem.at[i])
        for i, (src, dst) in enumerate(
            (
                (order, slots),
                (grad.at[0], strips),
                (left_inv.at[0], lr),
                (right_inv.at[0], rr),
                (left_old.at[0], lf),
                (right_old.at[0], rf),
            )
        )
    ]
    loads[0].start()
    loads[1].start()

    barrier = pltpu.get_barrier_semaphore()

    def signal(sem, dev):
        pl.semaphore_signal(sem, inc=1, device_id=dev, device_id_type=MESH)

    for dy in (2, 1, n_y - 1):
        signal(barrier, (peer(dy, 0), mp))
    for dz in (1, n_z - 1):
        signal(barrier, (peer(0, dz), mp))
    for partner in partners:
        signal(barrier, (dp, partner))

    for load in loads[2:]:
        load.start()
    loads[0].wait()
    loads[1].wait()

    my_rows = pl.ds(pl.multiple_of(dp * rows, rows), rows)

    def gather(k):
        @pl.loop(0, n_dp, unroll=4)
        def _(d):
            stage[d * per + k] = strips[slots[d * per + k]]

        owned[k, my_rows, :] = stage[dp * per + k]

    def send(k, dst):
        pltpu.make_async_remote_copy(
            src_ref=stage.at[dst * per + k],
            dst_ref=owned.at[k, my_rows],
            send_sem=out_send,
            recv_sem=out_recv.at[k],
            device_id=(dst, mp),
            device_id_type=MESH,
        ).start()

    def send_near(k):
        for dz in (1, n_z - 1):
            send(k, peer(0, dz))
        for dy in range(1, n_y):
            send(k, peer(dy, 0))

    def relay(step):
        for dz in (1, n_z - 1):
            signal(news.at[step], (peer(0, dz), mp))

    gather(0)
    pl.semaphore_wait(barrier, n_y - 1 + 2 + len(partners))
    relay(0)
    send_near(0)
    for k in range(1, per):
        gather(k)
        send_near(k)
    for step in range(n_z // 2):
        pl.semaphore_wait(news.at[step], 2)
        if step + 1 < n_z // 2:
            relay(step + 1)
        dist = step + 1
        sides = (dist, n_z - dist) if 2 * dist < n_z else (dist,)
        for dz in sides:

            @pl.loop(1, n_y)
            def _(dy):
                send(0, peer(dy, dz))

        if dist + 1 <= n_z // 2:
            for dz in (dist + 1, n_z - dist - 1)[: 2 if 2 * dist + 2 < n_z else 1]:
                send(0, peer(0, dz))

    for k in range(1, per):

        @pl.loop(2, n_z - 1)
        def _(dz):
            send(k, peer(0, dz))

        @pl.loop(0, (n_y - 1) * (n_z - 1))
        def _(i):
            send(k, peer(1 + i // (n_z - 1), 1 + lax.rem(i, n_z - 1)))

    for load in loads[2:]:
        load.wait()

    @pl.loop(0, per)
    def _(k):
        others = owned.at[k, pl.ds(0, (n_dp - 1) * rows)]
        pltpu.make_async_copy(others, others, out_recv.at[k]).wait()

        applied = jnp.dot(lr[k], owned[k], preferred_element_type=jnp.float32).astype(jnp.bfloat16)
        cond[...] = jnp.dot(applied, rr[k], preferred_element_type=jnp.float32)
        wide = owned[k].astype(jnp.float32)
        grad_square = jnp.sum(wide * wide)
        cond_square = jnp.sum(cond[...] * cond[...])
        row = lax.broadcasted_iota(jnp.int32, (8, 128), 0)
        mine = jnp.where(row == 0, grad_square, cond_square)
        def trade(step, value):
            sums_out[k, step] = value
            copy = pltpu.make_async_remote_copy(
                src_ref=sums_out.at[k, step],
                dst_ref=sums_in.at[k, step],
                send_sem=sum_send.at[k, step],
                recv_sem=sum_recv.at[k, step],
                device_id=(dp, partners[step]),
                device_id_type=MESH,
            )
            copy.start()
            return copy

        copy = trade(0, mine)

        block = owned[k]
        gram_left = lax.dot_general(
            block, block, (((1,), (1,)), ((), ())), preferred_element_type=jnp.float32
        )
        left_new[k] = (factor_decay * lf[k].astype(jnp.float32) + coef * gram_left).astype(
            jnp.bfloat16
        )
        gram_right = lax.dot_general(
            block, block, (((0,), (0,)), ((), ())), preferred_element_type=jnp.float32
        )
        right_new[k] = (factor_decay * rf[k].astype(jnp.float32) + coef * gram_right).astype(
            jnp.bfloat16
        )

        for step in range(len(partners)):
            copy.wait()
            total = sums_out[k, step] + sums_in[k, step]
            if step + 1 < len(partners):
                copy = trade(step + 1, total)
        graft = jnp.sqrt((total[0:1, 0:1] + epsilon) / (total[1:2, 0:1] + epsilon))
        update[k] = (-graft * cond[...]).astype(jnp.bfloat16)
        returned[dp * per + k] = update[k, my_rows, :]

        def send_back(dst):
            pltpu.make_async_remote_copy(
                src_ref=update.at[k, pl.ds(pl.multiple_of(dst * rows, rows), rows)],
                dst_ref=returned.at[dp * per + k],
                send_sem=back_send,
                recv_sem=back_recv,
                device_id=(dst, mp),
                device_id_type=MESH,
            ).start()

        for chosen in (
            lambda yy, zz: (zz < EARLY) & (yy == 0),
            lambda yy, zz: (zz < EARLY) & (yy != 0),
            lambda yy, zz: (zz == EARLY) | (zz == n_z - 1),
            lambda yy, zz: (zz > EARLY) & (zz < n_z - 1),
        ):

            @pl.loop(1, n_dp)
            def _(j):
                dst = lax.rem(dp + j, n_dp)

                @pl.when(chosen(dst // n_z, lax.rem(dst, n_z)))
                def _():
                    send_back(dst)

    others = (n_dp - 1) * per
    for sem in (out_send, back_send):
        pltpu.make_async_copy(
            stage.at[pl.ds(0, others)], stage.at[pl.ds(0, others)], sem
        ).wait()
    arrived = returned.at[pl.ds(0, others)]
    pltpu.make_async_copy(arrived, arrived, back_recv).wait()


def finish_kernel(
    order, returned, left, right, update, left_next, right_next, slots, placed, sem
):
    copies = [
        pltpu.make_async_copy(order, slots, sem.at[0]),
        pltpu.make_async_copy(left, left_next.at[0], sem.at[1]),
        pltpu.make_async_copy(right, right_next.at[0], sem.at[2]),
        pltpu.make_async_copy(placed, update.at[0], sem.at[3]),
    ]
    for copy in copies[:3]:
        copy.start()
    copies[0].wait()

    @pl.loop(0, placed.shape[0], unroll=4)
    def _(p):
        placed[slots[p]] = returned[p]

    copies[3].start()
    for copy in copies[1:]:
        copy.wait()


def body(n_dp, gradient, owner_order, left_factor, right_factor, left_root, right_root):
    _, blocks, rows, size = gradient.shape
    per = left_factor.shape[1]
    bf16, f32 = jnp.bfloat16, jnp.float32
    strips = (blocks, rows, size)
    squares = (per, size, size)
    any_spec = pl.BlockSpec(memory_space=pl.ANY)
    vmem_spec = pl.BlockSpec(memory_space=pltpu.VMEM)
    far = lambda x: pltpu.with_memory_space_constraint(x, pltpu.HBM)
    macs = 4 * per * size**3
    moved = gradient.size * 2
    returned, left_new, right_new = pl.pallas_call(
        functools.partial(exchange_kernel, (n_dp, per, rows)),
        out_shape=[
            pltpu.VMEM(strips, bf16),
            pltpu.VMEM(squares, bf16),
            pltpu.VMEM(squares, bf16),
        ],
        in_specs=[any_spec] * 6,
        out_specs=[vmem_spec] * 3,
        scratch_shapes=[
            pltpu.VMEM(strips, bf16),
            pltpu.VMEM(strips, bf16),
            pltpu.VMEM(squares, bf16),
            pltpu.SMEM((blocks,), jnp.int32),
            pltpu.VMEM(squares, bf16),
            pltpu.VMEM(squares, bf16),
            pltpu.VMEM(squares, bf16),
            pltpu.VMEM(squares, bf16),
            pltpu.VMEM((size, size), f32),
            pltpu.VMEM(squares, bf16),
            pltpu.VMEM((per, 3, 8, 128), f32),
            pltpu.VMEM((per, 3, 8, 128), f32),
            pltpu.SemaphoreType.REGULAR((RING // 2,)),
            pltpu.SemaphoreType.DMA((6,)),
            pltpu.SemaphoreType.DMA(()),
            pltpu.SemaphoreType.DMA((per,)),
            pltpu.SemaphoreType.DMA((per, 3)),
            pltpu.SemaphoreType.DMA((per, 3)),
            pltpu.SemaphoreType.DMA(()),
            pltpu.SemaphoreType.DMA(()),
        ],
        compiler_params=pltpu.CompilerParams(
            collective_id=0, has_side_effects=True, vmem_limit_bytes=40 << 20
        ),
        cost_estimate=pl.CostEstimate(
            flops=2 * macs, bytes_accessed=8 * moved, transcendentals=0
        ),
        name="exchange",
    )(
        far(gradient),
        far(owner_order),
        far(left_factor),
        far(right_factor),
        far(left_root),
        far(right_root),
    )

    keep = lambda x: pltpu.with_memory_space_constraint(x, pltpu.VMEM)
    return pl.pallas_call(
        finish_kernel,
        out_shape=[
            jax.ShapeDtypeStruct(gradient.shape, bf16),
            jax.ShapeDtypeStruct((1,) + squares, bf16),
            jax.ShapeDtypeStruct((1,) + squares, bf16),
        ],
        in_specs=[any_spec] + [vmem_spec] * 3,
        out_specs=[any_spec] * 3,
        scratch_shapes=[
            pltpu.SMEM((blocks,), jnp.int32),
            pltpu.VMEM(strips, bf16),
            pltpu.SemaphoreType.DMA((4,)),
        ],
        compiler_params=pltpu.CompilerParams(vmem_limit_bytes=16 << 20),
        cost_estimate=pl.CostEstimate(flops=0, bytes_accessed=6 * moved, transcendentals=0),
        name="finish",
    )(far(owner_order), keep(returned), keep(left_new), keep(right_new))


def solution(mesh):
    return jax.shard_map(
        functools.partial(body, mesh.shape["dp"]),
        mesh=mesh,
        in_specs=(
            P("mp", None, "dp", None),
            P(),
            P("mp", "dp", None, None),
            P("mp", "dp", None, None),
            P("mp", "dp", None, None),
            P("mp", "dp", None, None),
        ),
        out_specs=(P("mp", None, "dp", None), P("mp", "dp", None, None), P("mp", "dp", None, None)),
        check_vma=False,
    )
```

```python
import functools

import jax
import jax.numpy as jnp
from jax import lax
from jax.experimental import pallas as pl
from jax.experimental.pallas import tpu as pltpu
from jax.sharding import PartitionSpec as P

MESH = pl.DeviceIdType.MESH
factor_decay = 0.9
epsilon = 1e-06
RING = 8
EARLY = 3


def exchange_kernel(
    sizes,
    grad,
    order,
    left_old,
    right_old,
    left_inv,
    right_inv,
    returned,
    left_new,
    right_new,
    strips,
    stage,
    owned,
    slots,
    lf,
    rf,
    lr,
    rr,
    cond,
    update,
    sums_out,
    sums_in,
    news,
    load_sem,
    out_send,
    out_recv,
    sum_send,
    sum_recv,
    back_send,
    back_recv,
):
    n_dp, per, rows = sizes
    n_y, n_z = n_dp // RING, RING
    blocks = n_dp * per
    size = owned.shape[-1]
    dp = lax.axis_index("dp")
    mp = lax.axis_index("mp")
    coef = (1.0 - factor_decay) / size
    y, z = dp // n_z, lax.rem(dp, n_z)
    x, core = mp // 2, lax.rem(mp, 2)
    partners = (2 * x + 1 - core, 2 * (x + 1 - 2 * lax.rem(x, 2)) + core, 2 * (3 - x) + core)

    def peer(dy, dz):
        return lax.rem(y + dy, n_y) * n_z + lax.rem(z + dz, n_z)

    loads = [
        pltpu.make_async_copy(src, dst, load_sem.at[i])
        for i, (src, dst) in enumerate(
            (
                (order, slots),
                (grad.at[0], strips),
                (left_inv.at[0], lr),
                (right_inv.at[0], rr),
                (left_old.at[0], lf),
                (right_old.at[0], rf),
            )
        )
    ]
    loads[0].start()
    loads[1].start()

    barrier = pltpu.get_barrier_semaphore()

    def signal(sem, dev):
        pl.semaphore_signal(sem, inc=1, device_id=dev, device_id_type=MESH)

    for dy in (2, 1, n_y - 1):
        signal(barrier, (peer(dy, 0), mp))
    for dz in (1, n_z - 1):
        signal(barrier, (peer(0, dz), mp))
    for partner in partners:
        signal(barrier, (dp, partner))

    loads[0].wait()
    loads[1].wait()

    my_rows = pl.ds(pl.multiple_of(dp * rows, rows), rows)

    def gather(k):
        @pl.loop(0, n_dp, unroll=4)
        def _(d):
            stage[d * per + k] = strips[slots[d * per + k]]

        owned[k, my_rows, :] = stage[dp * per + k]

    def send(k, dst):
        pltpu.make_async_remote_copy(
            src_ref=stage.at[dst * per + k],
            dst_ref=owned.at[k, my_rows],
            send_sem=out_send,
            recv_sem=out_recv.at[k],
            device_id=(dst, mp),
            device_id_type=MESH,
        ).start()

    def send_near(k):
        for dz in (1, n_z - 1):
            send(k, peer(0, dz))
        for dy in range(1, n_y):
            send(k, peer(dy, 0))

    def relay(step):
        for dz in (1, n_z - 1):
            signal(news.at[step], (peer(0, dz), mp))

    gather(0)
    pl.semaphore_wait(barrier, n_y - 1 + 2 + len(partners))
    relay(0)
    send_near(0)
    for load in loads[2:]:
        load.start()
    for k in range(1, per):
        gather(k)
        send_near(k)
    for step in range(n_z // 2):
        pl.semaphore_wait(news.at[step], 2)
        if step + 1 < n_z // 2:
            relay(step + 1)
        dist = step + 1
        sides = (dist, n_z - dist) if 2 * dist < n_z else (dist,)
        for dz in sides:

            @pl.loop(1, n_y)
            def _(dy):
                send(0, peer(dy, dz))

        if dist + 1 <= n_z // 2:
            for dz in (dist + 1, n_z - dist - 1)[: 2 if 2 * dist + 2 < n_z else 1]:
                send(0, peer(0, dz))

    for k in range(1, per):

        @pl.loop(2, n_z - 1)
        def _(dz):
            send(k, peer(0, dz))

        @pl.loop(0, (n_y - 1) * (n_z - 1))
        def _(i):
            send(k, peer(1 + i // (n_z - 1), 1 + lax.rem(i, n_z - 1)))

    for load in loads[2:]:
        load.wait()

    @pl.loop(0, per)
    def _(k):
        others = owned.at[k, pl.ds(0, (n_dp - 1) * rows)]
        pltpu.make_async_copy(others, others, out_recv.at[k]).wait()

        applied = jnp.dot(lr[k], owned[k], preferred_element_type=jnp.float32).astype(jnp.bfloat16)
        cond[...] = jnp.dot(applied, rr[k], preferred_element_type=jnp.float32)
        wide = owned[k].astype(jnp.float32)
        grad_square = jnp.sum(wide * wide)
        cond_square = jnp.sum(cond[...] * cond[...])
        row = lax.broadcasted_iota(jnp.int32, (8, 128), 0)
        mine = jnp.where(row == 0, grad_square, cond_square)
        def trade(step, value):
            sums_out[k, step] = value
            copy = pltpu.make_async_remote_copy(
                src_ref=sums_out.at[k, step],
                dst_ref=sums_in.at[k, step],
                send_sem=sum_send.at[k, step],
                recv_sem=sum_recv.at[k, step],
                device_id=(dp, partners[step]),
                device_id_type=MESH,
            )
            copy.start()
            return copy

        copy = trade(0, mine)

        block = owned[k]
        gram_left = lax.dot_general(
            block, block, (((1,), (1,)), ((), ())), preferred_element_type=jnp.float32
        )
        left_new[k] = (factor_decay * lf[k].astype(jnp.float32) + coef * gram_left).astype(
            jnp.bfloat16
        )
        gram_right = lax.dot_general(
            block, block, (((0,), (0,)), ((), ())), preferred_element_type=jnp.float32
        )
        right_new[k] = (factor_decay * rf[k].astype(jnp.float32) + coef * gram_right).astype(
            jnp.bfloat16
        )

        for step in range(len(partners)):
            copy.wait()
            total = sums_out[k, step] + sums_in[k, step]
            if step + 1 < len(partners):
                copy = trade(step + 1, total)
        graft = jnp.sqrt((total[0:1, 0:1] + epsilon) / (total[1:2, 0:1] + epsilon))
        update[k] = (-graft * cond[...]).astype(jnp.bfloat16)
        returned[dp * per + k] = update[k, my_rows, :]

        def send_back(dst):
            pltpu.make_async_remote_copy(
                src_ref=update.at[k, pl.ds(pl.multiple_of(dst * rows, rows), rows)],
                dst_ref=returned.at[dp * per + k],
                send_sem=back_send,
                recv_sem=back_recv,
                device_id=(dst, mp),
                device_id_type=MESH,
            ).start()

        for chosen in (
            lambda yy, zz: (zz < EARLY) & (yy == 0),
            lambda yy, zz: (zz < EARLY) & (yy != 0),
            lambda yy, zz: (zz == EARLY) | (zz == n_z - 1),
            lambda yy, zz: (zz > EARLY) & (zz < n_z - 1),
        ):

            @pl.loop(1, n_dp)
            def _(j):
                dst = lax.rem(dp + j, n_dp)

                @pl.when(chosen(dst // n_z, lax.rem(dst, n_z)))
                def _():
                    send_back(dst)

    others = (n_dp - 1) * per
    for sem in (out_send, back_send):
        pltpu.make_async_copy(
            stage.at[pl.ds(0, others)], stage.at[pl.ds(0, others)], sem
        ).wait()
    arrived = returned.at[pl.ds(0, others)]
    pltpu.make_async_copy(arrived, arrived, back_recv).wait()


def finish_kernel(
    order, returned, left, right, update, left_next, right_next, slots, placed, sem
):
    copies = [
        pltpu.make_async_copy(order, slots, sem.at[0]),
        pltpu.make_async_copy(left, left_next.at[0], sem.at[1]),
        pltpu.make_async_copy(right, right_next.at[0], sem.at[2]),
        pltpu.make_async_copy(placed, update.at[0], sem.at[3]),
    ]
    for copy in copies[:3]:
        copy.start()
    copies[0].wait()

    @pl.loop(0, placed.shape[0], unroll=4)
    def _(p):
        placed[slots[p]] = returned[p]

    copies[3].start()
    for copy in copies[1:]:
        copy.wait()


def body(n_dp, gradient, owner_order, left_factor, right_factor, left_root, right_root):
    _, blocks, rows, size = gradient.shape
    per = left_factor.shape[1]
    bf16, f32 = jnp.bfloat16, jnp.float32
    strips = (blocks, rows, size)
    squares = (per, size, size)
    any_spec = pl.BlockSpec(memory_space=pl.ANY)
    vmem_spec = pl.BlockSpec(memory_space=pltpu.VMEM)
    far = lambda x: pltpu.with_memory_space_constraint(x, pltpu.HBM)
    macs = 4 * per * size**3
    moved = gradient.size * 2
    returned, left_new, right_new = pl.pallas_call(
        functools.partial(exchange_kernel, (n_dp, per, rows)),
        out_shape=[
            pltpu.VMEM(strips, bf16),
            pltpu.VMEM(squares, bf16),
            pltpu.VMEM(squares, bf16),
        ],
        in_specs=[any_spec] * 6,
        out_specs=[vmem_spec] * 3,
        scratch_shapes=[
            pltpu.VMEM(strips, bf16),
            pltpu.VMEM(strips, bf16),
            pltpu.VMEM(squares, bf16),
            pltpu.SMEM((blocks,), jnp.int32),
            pltpu.VMEM(squares, bf16),
            pltpu.VMEM(squares, bf16),
            pltpu.VMEM(squares, bf16),
            pltpu.VMEM(squares, bf16),
            pltpu.VMEM((size, size), f32),
            pltpu.VMEM(squares, bf16),
            pltpu.VMEM((per, 3, 8, 128), f32),
            pltpu.VMEM((per, 3, 8, 128), f32),
            pltpu.SemaphoreType.REGULAR((RING // 2,)),
            pltpu.SemaphoreType.DMA((6,)),
            pltpu.SemaphoreType.DMA(()),
            pltpu.SemaphoreType.DMA((per,)),
            pltpu.SemaphoreType.DMA((per, 3)),
            pltpu.SemaphoreType.DMA((per, 3)),
            pltpu.SemaphoreType.DMA(()),
            pltpu.SemaphoreType.DMA(()),
        ],
        compiler_params=pltpu.CompilerParams(
            collective_id=0, has_side_effects=True, vmem_limit_bytes=40 << 20
        ),
        cost_estimate=pl.CostEstimate(
            flops=2 * macs, bytes_accessed=8 * moved, transcendentals=0
        ),
        name="exchange",
    )(
        far(gradient),
        far(owner_order),
        far(left_factor),
        far(right_factor),
        far(left_root),
        far(right_root),
    )

    keep = lambda x: pltpu.with_memory_space_constraint(x, pltpu.VMEM)
    return pl.pallas_call(
        finish_kernel,
        out_shape=[
            jax.ShapeDtypeStruct(gradient.shape, bf16),
            jax.ShapeDtypeStruct((1,) + squares, bf16),
            jax.ShapeDtypeStruct((1,) + squares, bf16),
        ],
        in_specs=[any_spec] + [vmem_spec] * 3,
        out_specs=[any_spec] * 3,
        scratch_shapes=[
            pltpu.SMEM((blocks,), jnp.int32),
            pltpu.VMEM(strips, bf16),
            pltpu.SemaphoreType.DMA((4,)),
        ],
        compiler_params=pltpu.CompilerParams(vmem_limit_bytes=16 << 20),
        cost_estimate=pl.CostEstimate(flops=0, bytes_accessed=6 * moved, transcendentals=0),
        name="finish",
    )(far(owner_order), keep(returned), keep(left_new), keep(right_new))


def solution(mesh):
    return jax.shard_map(
        functools.partial(body, mesh.shape["dp"]),
        mesh=mesh,
        in_specs=(
            P("mp", None, "dp", None),
            P(),
            P("mp", "dp", None, None),
            P("mp", "dp", None, None),
            P("mp", "dp", None, None),
            P("mp", "dp", None, None),
        ),
        out_specs=(P("mp", None, "dp", None), P("mp", "dp", None, None), P("mp", "dp", None, None)),
        check_vma=False,
    )
```
